256 devices in a mesh: req: 32 (over y, x, core), samp: 8 (over z).
Axes of the slice: x: 4, y: 4, z: 8, core: 2. Of those that a mesh axis runs over, the one named last changes fastest.
Arguments:
- features: bfloat16 [49152, 7168], P('req', 'samp'), may hold values from -6 to 6
- gate_input: bfloat16 [49152, 7168], P('req', 'samp'), may hold values from -15.5 to 15.5
- input_map: bfloat16 [49152, 128], P('req'), may hold values from -6 to 6
- output_map: bfloat16 [49152, 128], P('req'), may hold values from -6 to 6
- head_step_sizes: float32 [112, 49152], P('samp', 'req'), may hold values from 0.0005 to 0.6, as said below
- log_rate: float32 [112], P('samp'), may hold values from -0.35 to 0.35
- skip_gain: float32 [112], P('samp'), may hold values from 0.5 to 1.5
- norm_gain: float32 [7168], P('samp'), may hold values from 0.5 to 1.5
- cache_states: bfloat16 [512, 112, 4096], P('req', 'samp'), may hold values from -3 to 3
- hit_owner: int32 [512, 1], P('req'), may hold values from 0 to 31; in each aligned block of 16 rows (0 to 15, 16 to 31, ...) at most 2 rows name the same one
- hit_slot: int32 [512], P('req'), may hold values from 0 to 15
- suffix_blocks: int32 [32, 16], P('req'), may hold values from 1 to 4, 24 in all within a row
- dec_features: bfloat16 [512, 8, 2, 7168], P('req', None, None, 'samp'), may hold values from -6 to 6
- dec_gate: bfloat16 [512, 8, 2, 7168], P('req', None, None, 'samp'), may hold values from -15.5 to 15.5
- dec_input_map: bfloat16 [512, 8, 2, 128], P('req'), may hold values from -6 to 6
- dec_output_map: bfloat16 [512, 8, 2, 128], P('req'), may hold values from -6 to 6
- dec_step_size: float32 [112, 512, 8, 2], P('samp', 'req'), may hold values from 0.0005 to 0.6, as said below
Outputs:
- prefill_out: bfloat16 [49152, 7168], P('req', 'samp')
- decode_out: bfloat16 [512, 8, 2, 7168], P('req', None, None, 'samp')
The draws below stay inside these ranges and needn't reach their ends.
Inputs may be any that keep to these rules, and one draw needn't show every extreme that they name: `hit_owner`: among the 16 requests of one device, at most 2 name the same owner, and some owner is named by 2 of them. `suffix_blocks`: each row sums to 24. `head_step_sizes`: Positive. `dec_step_size`: Positive.
All inputs are finite; a program needn't handle non-finite values.
Results may differ from the reference program's by a relative error of at most 0.0034.
Values may be sent and summed in bfloat16 or wider, within the bound.
No kernel may reach another device: no remote copies, remote signals or barrier semaphores. Data moves between devices by JAX's collectives and lax.ppermute only.
A program may use at most 192 MiB of HBM per device.

```python
import math
import jax
import jax.numpy as jnp
import numpy as np
from jax import lax

HEADS = 112
HEAD_DIM = 64
STATE = 64
GROUPS = 2
BLOCK_LEN = 64
MOST = 4
CAP = 2
STEPS = 2
REQUESTS_PER_UNIT = 16
BLOCKS_DEV = 16
SAMPLES = 8
D_INNER = 7168
CH_DEV = 24
TOK_DEV = 1536
TOKENS = 49152
REQUESTS = 512
MEMO_STATE_COUNT = 512
N_REQ = 32


def head_rates(key, quick_share):
    pick = jax.random.uniform(jax.random.fold_in(key, 101), (HEADS,))
    quick = jax.random.uniform(jax.random.fold_in(key, 102), (HEADS,), minval=jnp.log(0.03), maxval=jnp.log(0.05))
    steady = jax.random.uniform(jax.random.fold_in(key, 103), (HEADS,), minval=jnp.log(0.001), maxval=jnp.log(0.004))
    return jnp.exp(jnp.where(pick < quick_share, quick, steady))


def rough_steps(key, starting_position, dimension_list):
    coarse_guess = jax.random.uniform(jax.random.fold_in(key, 1), dimension_list, minval=0.7, maxval=1.4)
    spell_interval = jax.random.uniform(jax.random.fold_in(key, 2), dimension_list) < 1.0 / 256.0
    surplus_quantity = jax.random.uniform(jax.random.fold_in(key, 3), dimension_list, minval=0.32, maxval=0.48)
    return starting_position * coarse_guess + jnp.where(spell_interval, surplus_quantity, 0.0)


def ramped(values):
    channel = jnp.arange(D_INNER).astype(jnp.float32)
    return values * (1.0 + 2.0 * channel / (D_INNER - 1))


def draw_head_step_sizes(key, part):
    starting_position = head_rates(key, 0.5)
    key = jax.random.fold_in(key, 7)
    return rough_steps(key, starting_position[:, None], (HEADS, TOKENS))


def draw_dec_step_size(key, part):
    starting_position = head_rates(key, 0.5)
    key = jax.random.fold_in(key, 8)
    return rough_steps(key, starting_position[:, None, None, None], (HEADS, REQUESTS, SAMPLES, STEPS))


def draw_gate_input(key, part):
    key = jax.random.fold_in(key, 11)
    dimension_list = (TOKENS, D_INNER)
    return ramped(jnp.clip(jax.random.normal(jax.random.fold_in(key, 2), dimension_list), -5.0, 5.0)).astype(jnp.bfloat16)


def draw_dec_gate(key, part):
    key = jax.random.fold_in(key, 12)
    dimension_list = (REQUESTS, SAMPLES, STEPS, D_INNER)
    return ramped(jnp.clip(jax.random.normal(jax.random.fold_in(key, 2), dimension_list), -5.0, 5.0)).astype(jnp.bfloat16)


def set_ends(entries, rng, least, high):
    longest = entries.shape.index(max(entries.shape))
    spots = []
    for shift in (0, 1):
        where = [jax.random.randint(jax.random.fold_in(rng, axis), (), 0, length) for axis, length in enumerate(entries.shape)]
        where[longest] = (where[longest] + shift) % entries.shape[longest]
        spots.append(tuple(where))
    return entries.at[spots[0]].set(least).at[spots[1]].set(high)


def block_levels(own_key, shape, pieces, smallest, top_value):
    factor_of = 1.0
    for axis_at, parts in pieces:
        draws = jax.random.uniform(jax.random.fold_in(jax.random.fold_in(own_key, 6), axis_at), (parts,), jnp.float32, smallest / len(pieces), top_value / len(pieces))
        factor_of = factor_of * jnp.repeat(jnp.exp(draws), shape[axis_at] // parts).reshape((-1,) + (1,) * (len(shape) - 1 - axis_at))
    return factor_of


def profile(number_of, total, limit, skew):
    weights = [(1 << 20) // math.isqrt(standing ** skew) + 1 for standing in range(2, number_of + 1)]
    surplus, given = total - limit - (number_of - 1), [1] * (number_of - 1)
    while surplus > 0:
        movable = [i for i in range(number_of - 1) if given[i] < limit]
        pool, budget = sum([weights[i] for i in movable]), surplus
        for i in movable:
            addition = min(limit - given[i], max(1, budget * weights[i] // pool), surplus)
            given[i] = given[i] + addition
            surplus = surplus - addition
    return np.array([limit] + given)


def uneven_parts(rng, number_of, total, limit, skew):
    if number_of == 2:
        one = jax.random.randint(rng, (), max(1, total - limit), min(limit, total - 1) + 1)
        return jnp.stack([one, total - one])
    sizes = jnp.asarray(profile(number_of, total, limit, skew), jnp.int32)
    twos = (number_of - 1) // 2
    giver, sink = sizes[1:1 + 2 * twos:2], sizes[2:2 + 2 * twos:2]
    margin = jnp.minimum(giver - 1, limit - sink)
    shifted = jax.random.randint(jax.random.fold_in(rng, 1), (twos,), 0, 1 << 20) % (margin + 1)
    sizes = sizes.at[1:1 + 2 * twos:2].set(giver - shifted).at[2:2 + 2 * twos:2].set(sink + shifted)
    return sizes[jax.random.permutation(jax.random.fold_in(rng, 2), number_of)]


def assign_block(stream_key, own, number, rows, amount, top, bound, slope):
    sequence = jax.random.permutation(stream_key, amount)
    packed, ordinary = portions_of(amount, rows * top, bound, slope, True), portions_of(amount, rows * top, bound, slope, False)
    places = jnp.arange(amount)

    def named(lengths, offset_by):
        used = int((lengths > 0).sum())
        fixed = max(1, used // 4)
        passed = fixed + (places - fixed + offset_by * (used - fixed)) % max(1, amount - fixed)
        return jnp.zeros((amount,), jnp.int32).at[sequence[jnp.where(places < fixed, places, passed)]].set(jnp.asarray(lengths, jnp.int32))

    lengths = jnp.where(number % 4 == 0, named(packed, number // 4), named(ordinary, number - number // 4 - 1))
    mixed = jax.random.permutation(jax.random.fold_in(own, 3), amount)
    donor, taker = mixed[0:amount // 2 * 2:2], mixed[1:amount // 2 * 2:2]
    room = jnp.minimum(lengths[donor] - 1, bound - lengths[taker]) // 2
    room = jnp.where((donor == sequence[0]) | (taker == sequence[0]) | (lengths[taker] == 0), 0, jnp.maximum(room, 0))
    passed = jax.random.randint(jax.random.fold_in(own, 4), (amount // 2,), 0, 1 << 20) % (room + 1)
    lengths = lengths.at[donor].add(-passed).at[taker].add(passed)
    items = jnp.searchsorted(jnp.cumsum(lengths), jnp.arange(rows * top), side="right").astype(jnp.int32)
    listing = items.reshape(top, rows).T
    listing = listing[jax.random.permutation(jax.random.fold_in(own, 1), rows)]
    offset_by = jax.random.randint(jax.random.fold_in(own, 2), (rows, 1), 0, top)
    return jnp.take_along_axis(listing, (jnp.arange(top)[None, :] + offset_by) % top, axis=1)


def portions_of(count, total, bound, lean, full):
    portions = [(1 << 20) // math.isqrt(grade ** lean) + 1 for grade in range(1, count + 1)]
    largest = bound if full else min(bound, max(-(-total // count), total * portions[0] // sum(portions)))
    least = 1 if total - largest >= count - 1 else 0
    holding, rest = [largest] + [least] * (count - 1), total - largest - least * (count - 1)
    while rest > 0:
        movable = [i for i in range(1, count) if holding[i] < largest] or [i for i in range(1, count) if holding[i] < bound]
        mass, left = sum([portions[i] for i in movable]), rest
        for i in movable:
            extra = min(bound - holding[i], max(1, left * portions[i] // mass), rest)
            holding[i] = holding[i] + extra
            rest = rest - extra
    return np.array(holding)


def gaussian(stream_key, extent, width, bound, pieces=(), held_as=jnp.bfloat16):
    drawn = jax.random.normal(stream_key, extent, jnp.float32) * width
    if len(pieces) > 0:
        drawn = block_levels(stream_key, extent, pieces, -0.22, 0.18) * drawn
    return jnp.clip(drawn, min=-bound, max=bound).astype(held_as)


def setup_inputs(seed: int = 0) -> dict:
    splits = jax.random.split(jax.random.key(seed), 18)
    features = gaussian(splits[0], (TOKENS, D_INNER), 1.0, 6.0, ((0, 32), (1, 8)))
    gate_input = draw_gate_input(jax.random.fold_in(splits[17], 71), 0)
    input_map = gaussian(splits[2], (TOKENS, GROUPS * STATE), 1.0, 6.0, ((0, 32),))
    output_map = gaussian(splits[3], (TOKENS, GROUPS * STATE), 1.0, 6.0, ((0, 32),))
    head_step_sizes = draw_head_step_sizes(jax.random.fold_in(splits[17], 71), 0)
    log_rate = jnp.clip(jax.random.uniform(splits[5], (HEADS,), jnp.float32, -0.35, 0.35) * block_levels(splits[5], (HEADS,), ((0, 8),), -0.4, 0.0), -0.35, 0.35)
    skip_gain = jnp.clip(0.5 + 1.0 * jax.random.uniform(splits[6], (HEADS,), jnp.float32) ** block_levels(splits[6], (HEADS,), ((0, 8),), -0.2, 0.2), 0.5, 1.5)
    norm_gain = jnp.clip(1.0 + 0.1 * jax.random.normal(splits[7], (D_INNER,), jnp.float32), 0.5, 1.5)
    cache_states = gaussian(splits[8], (MEMO_STATE_COUNT, HEADS, HEAD_DIM * STATE), 0.5, 3.0, ((0, 32), (1, 8)))
    hit_owner_keys = jax.random.split(jax.random.fold_in(splits[9], 1), REQUESTS // REQUESTS_PER_UNIT)
    hit_owner_turns = jax.random.permutation(jax.random.fold_in(splits[9], 3), REQUESTS // REQUESTS_PER_UNIT)
    hit_owner = jax.vmap(lambda own, number: assign_block(jax.random.fold_in(splits[9], 2), own, number, REQUESTS_PER_UNIT, N_REQ, 1, CAP, 2))(hit_owner_keys, hit_owner_turns).reshape((REQUESTS, 1))
    hit_slot = set_ends(jax.random.randint(splits[10], (REQUESTS,), 0, BLOCKS_DEV), jax.random.fold_in(splits[10], 1), 0, BLOCKS_DEV - 1).astype(jnp.int32)
    suffix_blocks = jax.vmap(lambda own: uneven_parts(own, REQUESTS_PER_UNIT, CH_DEV, MOST, 1))(jax.random.split(splits[11], N_REQ)).reshape((N_REQ, REQUESTS_PER_UNIT)).astype(jnp.int32)
    dec_features = gaussian(splits[12], (REQUESTS, SAMPLES, STEPS, D_INNER), 1.0, 6.0, ((0, 32), (3, 8)))
    dec_gate = draw_dec_gate(jax.random.fold_in(splits[17], 71), 0)
    dec_input_map = gaussian(splits[14], (REQUESTS, SAMPLES, STEPS, GROUPS * STATE), 1.0, 6.0, ((0, 32),))
    dec_output_map = gaussian(splits[15], (REQUESTS, SAMPLES, STEPS, GROUPS * STATE), 1.0, 6.0, ((0, 32),))
    dec_step_size = draw_dec_step_size(jax.random.fold_in(splits[17], 71), 0)
    return {"features": features, "gate_input": gate_input, "input_map": input_map, "output_map": output_map, "head_step_sizes": head_step_sizes, "log_rate": log_rate, "skip_gain": skip_gain, "norm_gain": norm_gain, "cache_states": cache_states, "hit_owner": hit_owner, "hit_slot": hit_slot, "suffix_blocks": suffix_blocks, "dec_features": dec_features, "dec_gate": dec_gate, "dec_input_map": dec_input_map, "dec_output_map": dec_output_map, "dec_step_size": dec_step_size}


HIGH = lax.Precision.HIGHEST

def gated_norm_output(values, gate, gain):
    gated = values * jax.nn.silu(gate.astype(jnp.float32))
    mean = lax.optimization_barrier(jnp.mean(gated * gated, axis=-1, keepdims=True))
    normed = gated * lax.rsqrt(mean + 1e-05)
    return (normed * gain).astype(jnp.bfloat16)

def prefill_block(xval, bval, cval, steps, log_rate, skip_gain, initial, lens):
    nblk = TOK_DEV // BLOCK_LEN
    group_of = jnp.arange(HEADS, dtype=jnp.int32) // (HEADS // GROUPS)
    logd = -(steps * jnp.exp(log_rate)[:, None]).reshape(HEADS, nblk, BLOCK_LEN)
    cums = jnp.cumsum(logd, axis=2)
    dtc = steps.reshape(HEADS, nblk, BLOCK_LEN)
    xc = xval.reshape(nblk, BLOCK_LEN, HEADS, HEAD_DIM).astype(jnp.float32)
    bc = bval.reshape(nblk, BLOCK_LEN, GROUPS, STATE).astype(jnp.float32)
    cc = cval.reshape(nblk, BLOCK_LEN, GROUPS, STATE).astype(jnp.float32)
    gram = jnp.einsum('ktgn,ksgn->gkts', cc, bc, precision=HIGH)[group_of]
    lower = jnp.arange(BLOCK_LEN)[None, :] <= jnp.arange(BLOCK_LEN)[:, None]
    gap = jnp.where(lower, cums[:, :, :, None] - cums[:, :, None, :], 0.0)
    weights = jnp.where(lower, jnp.exp(gap) * gram * dtc[:, :, None, :], 0.0).astype(jnp.bfloat16)
    weights = lax.optimization_barrier(weights).astype(jnp.float32)
    inner = jnp.einsum('hkts,kshp->kthp', weights, xc, precision=HIGH)
    tail = jnp.exp(cums[:, :, -1:] - cums) * dtc
    scaled = (xc * jnp.transpose(tail, (1, 2, 0))[..., None]).astype(jnp.bfloat16)
    scaled = lax.optimization_barrier(scaled).astype(jnp.float32)
    growth = jnp.einsum('kshp,kshn->khpn', scaled, bc[:, :, group_of, :], precision=HIGH)
    fade = jnp.transpose(jnp.exp(cums[:, :, -1]), (1, 0))
    ends = jnp.cumsum(lens).astype(jnp.int32)
    firsts = (ends - lens).astype(jnp.int32)
    index = jnp.arange(nblk, dtype=jnp.int32)[:, None]
    owner_req = lax.optimization_barrier(jnp.sum((ends[None, :] <= index).astype(jnp.int32), axis=1)).astype(jnp.int32)
    begins = jnp.any(firsts[None, :] == index, axis=1)

    def advance(carry, item):
        start, which, decay, add = item
        entry = jnp.where(start, initial[which], carry)
        leave = decay[:, None, None] * entry + add
        return (leave, (entry, leave))
    zero = jnp.zeros((HEADS, HEAD_DIM, STATE), jnp.float32)
    _, (entering, leaving) = lax.scan(advance, zero, (begins, owner_req, fade, growth))
    outer = jnp.einsum('kthn,khpn->kthp', cc[:, :, group_of, :], entering, precision=HIGH)
    outer = outer * jnp.exp(jnp.transpose(cums, (1, 2, 0)))[..., None]
    total = inner + outer + skip_gain[None, None, :, None] * xc
    finals = jnp.take(leaving, ends - 1, axis=0)
    return (total.reshape(TOK_DEV, D_INNER), finals)

def decode_block(finals, xval, bval, cval, steps, log_rate, skip_gain):
    group_of = jnp.arange(HEADS, dtype=jnp.int32) // (HEADS // GROUPS)
    rate = jnp.exp(log_rate)

    def one_request(item):
        state0, xr, br, cr, dtr = item
        state = jnp.broadcast_to(state0[None], (SAMPLES,) + state0.shape)
        outs = []
        for j in range(STEPS):
            step_j = jnp.transpose(dtr[:, :, j], (1, 0))
            keep = jnp.exp(-step_j * rate[None, :])
            xj = xr[:, j].reshape(SAMPLES, HEADS, HEAD_DIM).astype(jnp.float32)
            bj = br[:, j].reshape(SAMPLES, GROUPS, STATE).astype(jnp.float32)[:, group_of]
            cj = cr[:, j].reshape(SAMPLES, GROUPS, STATE).astype(jnp.float32)[:, group_of]
            state = keep[:, :, None, None] * state + (step_j[:, :, None] * xj)[..., None] * bj[:, :, None, :]
            reading = jnp.einsum('shpn,shn->shp', state, cj, precision=HIGH)
            outs.append(reading + skip_gain[None, :, None] * xj)
        return jnp.stack(outs, axis=1).reshape(SAMPLES, STEPS, D_INNER)
    return lax.map(one_request, (finals, xval, bval, cval, jnp.transpose(steps, (1, 0, 2, 3))))

def reference(features, gate_input, input_map, output_map, head_step_sizes, log_rate, skip_gain, norm_gain, cache_states, hit_owner, hit_slot, suffix_blocks, dec_features, dec_gate, dec_input_map, dec_output_map, dec_step_size):
    block_ids = (hit_owner[:, 0] * BLOCKS_DEV + hit_slot).astype(jnp.int32)

    def one_device(index):
        first_tok = index * TOK_DEV
        first_req = index * REQUESTS_PER_UNIT
        xval = lax.dynamic_slice_in_dim(features, first_tok, TOK_DEV, 0)
        zval = lax.dynamic_slice_in_dim(gate_input, first_tok, TOK_DEV, 0)
        bval = lax.dynamic_slice_in_dim(input_map, first_tok, TOK_DEV, 0)
        cval = lax.dynamic_slice_in_dim(output_map, first_tok, TOK_DEV, 0)
        steps = lax.dynamic_slice_in_dim(head_step_sizes, first_tok, TOK_DEV, 1)
        ids = lax.dynamic_slice_in_dim(block_ids, first_req, REQUESTS_PER_UNIT, 0)
        initial = jnp.take(cache_states, ids, axis=0).astype(jnp.float32).reshape(REQUESTS_PER_UNIT, HEADS, HEAD_DIM, STATE)
        lens = lax.dynamic_index_in_dim(suffix_blocks, index, 0, keepdims=False).astype(jnp.int32)
        values, finals = prefill_block(xval, bval, cval, steps, log_rate, skip_gain, initial, lens)
        pre = gated_norm_output(values, zval, norm_gain)
        dx = lax.dynamic_slice_in_dim(dec_features, first_req, REQUESTS_PER_UNIT, 0)
        dz = lax.dynamic_slice_in_dim(dec_gate, first_req, REQUESTS_PER_UNIT, 0)
        db = lax.dynamic_slice_in_dim(dec_input_map, first_req, REQUESTS_PER_UNIT, 0)
        dc = lax.dynamic_slice_in_dim(dec_output_map, first_req, REQUESTS_PER_UNIT, 0)
        dd = lax.dynamic_slice_in_dim(dec_step_size, first_req, REQUESTS_PER_UNIT, 1)
        dec_values = decode_block(finals, dx, db, dc, dd, log_rate, skip_gain)
        return (pre, gated_norm_output(dec_values, dz, norm_gain))
    pre, dec = lax.map(one_device, jnp.arange(N_REQ, dtype=jnp.int32))
    return (pre.reshape(TOKENS, D_INNER), dec.reshape(REQUESTS, SAMPLES, STEPS, D_INNER))
```

```python
import jax
import jax.numpy as jnp
import ml_dtypes
import numpy as np
from jax import lax
from jax.experimental import pallas as pl
from jax.experimental.pallas import tpu as pltpu
from jax.sharding import PartitionSpec as P

HEADS = 112
HEAD_DIM = 64
STATE = 64
GROUPS = 2
BLOCK_LEN = 64
CAP = 2
STEPS = 2
D_INNER = 7168

LOCAL = 14
WIDTH = LOCAL * HEAD_DIM
REQS = 16
OWNERS = 32
NBLK = 24
TOKS = NBLK * BLOCK_LEN
DEC = 16
ROWS = BLOCK_LEN + DEC
QUARTERS = 4
PIECE = STATE // QUARTERS
TILES = tuple(slice(i, min(i + 256, WIDTH)) for i in range(0, WIDTH, 256))
WIDE = 768
TWO = 2
FOUR = 4
PLACES = 3
SHIFTS = ((0, 1), (0, 3), (1, 0), (3, 0))

F32 = jnp.float32
BF16 = jnp.bfloat16
HIGH = lax.Precision.HIGHEST


def dot(a, b):
    return jnp.dot(a, b, preferred_element_type=F32)


def dot_nt(a, b):
    return lax.dot_general(a, b, (((1,), (1,)), ((), ())), preferred_element_type=F32)


def dot_tn(a, b):
    return lax.dot_general(a, b, (((0,), (0,)), ((), ())), preferred_element_type=F32)


def params(mib):
    return pltpu.CompilerParams(vmem_limit_bytes=mib << 20)


def spread_matrix():
    out = np.zeros((2, 32, REQS, REQS, HEAD_DIM), np.float32)
    for parity in range(2):
        for i in range(32):
            for slot in range(REQS):
                out[parity, i, slot, slot, 2 * i + parity] = 1.0
    return out.reshape(1024, 1024).astype(ml_dtypes.bfloat16)


def shifted(device, q):
    y, x, core = device >> 3, (device >> 1) & 3, device & 1
    step = 1 + 2 * (q & 1)
    dy = jnp.where(q >= 2, step, 0)
    dx = jnp.where(q >= 2, 0, step)
    return (((y + dy) & 3) << 3) + (((x + dx) & 3) << 1) + core


def choices(owner, q):
    return owner, owner ^ 1, shifted(owner, q)


def lightest(load, devices):
    a, b, c = (load[device] for device in devices)
    kind = jnp.where((a <= b) & (a <= c), 0, jnp.where(b <= c, 1, 2))
    device = jnp.where(kind == 0, devices[0], jnp.where(kind == 1, devices[1], devices[2]))
    return kind, device, jnp.minimum(a, jnp.minimum(b, c))


def make_plan(owners, slots, table, loc, load, held, seen, origin, queue, late):
    for device in range(OWNERS):
        load[device] = 0
        for place in range(PLACES):
            table[device, place] = 0
    for n in range(REQS * QUARTERS):
        loc[n] = 0

    def put(ball, kind, device, place):
        request, q = ball & 15, ball >> 4
        held[device * PLACES + place] = ball
        loc[request * QUARTERS + q] = device * PLACES + place
        table[device, place] = (kind << 6) + (q << 4) + slots[request]

    waiting = jnp.int32(0)
    for q in range(QUARTERS):
        for request in range(REQS):
            kind, best, room = lightest(load, choices(owners[request], q))
            fits = room < PLACES

            @pl.when(fits)
            def _():
                put((q << 4) + request, kind, best, room)
                load[best] = room + 1

            @pl.when(jnp.logical_not(fits))
            def _():
                late[waiting] = (q << 4) + request

            waiting = waiting + jnp.where(fits, 0, 1)

    def place_late(n, failed):
        ball = late[n]
        for device in range(OWNERS):
            seen[device] = 0

        def visit(options, source, state):
            tail, found = state
            for kind in range(3):
                device = options[kind]
                fresh = (seen[device] == 0) & (found < 0)

                @pl.when(fresh)
                def _():
                    seen[device] = 1
                    origin[device] = (source << 2) + kind
                    queue[tail] = device

                tail = tail + jnp.where(fresh, 1, 0)
                found = jnp.where(fresh & (load[device] < PLACES), device, found)
            return tail, found

        root = OWNERS * PLACES
        start = visit(choices(owners[ball & 15], ball >> 4), root, (jnp.int32(0), jnp.int32(-1)))

        def search(state):
            head, tail, found = state
            device = queue[head]
            for place in range(PLACES):
                spot = device * PLACES + place
                other = held[spot]
                tail, found = visit(choices(owners[other & 15], other >> 4), spot, (tail, found))
            return head + 1, tail, found

        _, _, found = lax.while_loop(
            lambda state: (state[0] < state[1]) & (state[2] < 0),
            search,
            (jnp.int32(0),) + start,
        )

        @pl.when(found >= 0)
        def _():
            room = load[found]
            load[found] = room + 1

            def back(state):
                device, place = state
                source, kind = origin[device] >> 2, origin[device] & 3
                first = source == root
                moved = jnp.where(first, ball, held[jnp.minimum(source, root - 1)])
                put(moved, kind, device, place)
                above = (source * 43) >> 7
                return jnp.where(first, -1, above), source - above * PLACES

            lax.while_loop(lambda state: state[0] >= 0, back, (found, room))

        return failed | jnp.where(found < 0, 1, 0)

    failed = lax.fori_loop(0, waiting, place_late, jnp.int32(0))
    for device in range(OWNERS):
        table[device, PLACES] = failed


def prepare_kernel(
    owners, slots, far_cache, far_spread,
    table, loc, whole, part0, part1, part2, part3,
    cache, spread, turned, load, held, seen, origin, queue, late, sems,
):
    copies = (
        pltpu.make_async_copy(far_cache, cache, sems.at[0]),
        pltpu.make_async_copy(far_spread, spread, sems.at[1]),
    )
    for copy in copies:
        copy.start()
    make_plan(owners, slots, table, loc, load, held, seen, origin, queue, late)
    for copy in copies:
        copy.wait()
    parts = (part0, part1, part2, part3)
    for head in range(LOCAL):
        for chunk in range(4):
            tiles = [
                cache[head, :, (8 * chunk + i) * 128 : (8 * chunk + i + 1) * 128] for i in range(8)
            ]
            block = jnp.concatenate(tiles, axis=0).T
            for parity in range(2):
                first = parity * 512 + chunk * 128
                turned[head * 64 : head * 64 + 64, first : first + 128] = block[
                    parity * 64 : parity * 64 + 64
                ]
    low = lax.broadcasted_iota(jnp.int32, (64, 128), 1) < 64
    for four in range(4):
        out = dot(turned[...], spread[:, four * 256 : four * 256 + 256])
        for two in range(2):
            for pair in range(LOCAL // 2):
                even = out[pair * 128 : pair * 128 + 64, two * 128 : two * 128 + 128]
                odd = out[pair * 128 + 64 : pair * 128 + 128, two * 128 : two * 128 + 128]
                first = jnp.where(low, even, pltpu.roll(odd, 64, 1)).astype(BF16)
                second = jnp.where(low, pltpu.roll(even, 64, 1), odd).astype(BF16)
                for one, value in ((0, first), (1, second)):
                    slot = four * 4 + two * 2 + one
                    for q in range(QUARTERS):
                        piece = value[q * PIECE : (q + 1) * PIECE]
                        whole[q, slot, :, pair * 128 : pair * 128 + 128] = piece
                        parts[q][slot, :, pair * 128 : pair * 128 + 128] = piece


def prepare(owners, slots, cache):
    smem = pl.BlockSpec(memory_space=pltpu.SMEM)
    vmem = pl.BlockSpec(memory_space=pltpu.VMEM)
    anywhere = pl.BlockSpec(memory_space=pl.ANY)
    piece = jax.ShapeDtypeStruct((REQS, PIECE, WIDTH), BF16)
    return pl.pallas_call(
        prepare_kernel,
        out_shape=[
            jax.ShapeDtypeStruct((OWNERS, 4), jnp.int32),
            jax.ShapeDtypeStruct((REQS * QUARTERS,), jnp.int32),
            jax.ShapeDtypeStruct((QUARTERS, REQS, PIECE, WIDTH), BF16),
        ]
        + [piece] * 4,
        in_specs=[smem, smem, anywhere, anywhere],
        out_specs=[smem] * 2 + [vmem] * 5,
        scratch_shapes=[
            pltpu.VMEM((LOCAL, REQS, HEAD_DIM * STATE), BF16),
            pltpu.VMEM((1024, 1024), BF16),
            pltpu.VMEM((LOCAL * 64, 1024), BF16),
            pltpu.SMEM((OWNERS,), jnp.int32),
            pltpu.SMEM((OWNERS * PLACES,), jnp.int32),
            pltpu.SMEM((OWNERS,), jnp.int32),
            pltpu.SMEM((OWNERS,), jnp.int32),
            pltpu.SMEM((OWNERS,), jnp.int32),
            pltpu.SMEM((REQS * QUARTERS,), jnp.int32),
            pltpu.SemaphoreType.DMA((2,)),
        ],
        compiler_params=params(60),
        name="prepare",
    )(owners, slots, jnp.transpose(cache, (1, 0, 2)), jnp.asarray(spread_matrix()))


def collect_kernel(table, own, peer, near0, near1, near2, near3, out, sem):
    near = (near0, near1, near2, near3)

    def each(device, _):
        for place in range(PLACES):
            code = table[device, place]
            kind, q, slot = code >> 6, (code >> 4) & 3, code & 15
            target = out.at[device * PLACES + place]

            @pl.when(kind == 0)
            def _():
                pltpu.make_async_copy(own.at[q, slot], target, sem).start()

            @pl.when(kind == 1)
            def _():
                pltpu.make_async_copy(peer.at[q, slot], target, sem).start()

            for side in range(QUARTERS):

                @pl.when((kind == 2) & (q == side))
                def _():
                    pltpu.make_async_copy(near[side].at[slot], target, sem).start()

        return 0

    lax.fori_loop(0, OWNERS, each, 0)
    pltpu.make_async_copy(out, out, sem).wait()


def collect(table, own, peer, near):
    vmem = pl.BlockSpec(memory_space=pltpu.VMEM)
    return pl.pallas_call(
        collect_kernel,
        out_shape=jax.ShapeDtypeStruct((OWNERS * PLACES, PIECE, WIDTH), BF16),
        in_specs=[pl.BlockSpec(memory_space=pltpu.SMEM)] + [vmem] * 6,
        out_specs=pl.BlockSpec(memory_space=pl.ANY),
        scratch_shapes=[pltpu.SemaphoreType.DMA],
        compiler_params=params(16),
        name="collect",
    )(table, own, peer, *near)


def silu(value):
    return value / (1.0 + jnp.exp(-value))


def thirds(value):
    high = value.astype(BF16).astype(F32)
    rest = value - high
    mid = rest.astype(BF16).astype(F32)
    return jnp.concatenate([high, mid, rest - mid], axis=0)


def before_kernel(
    req_of, x, z, b, c, dt, rates, skip, dx, dz, db, dc, dd, dprev, expand,
    base, slope, growth, left, fade, columns,
):
    @pl.when(pl.program_id(0) == 0)
    def _():
        columns[...] = jnp.zeros_like(columns)

    rate = jnp.exp(rates[...])
    rows = lax.broadcasted_iota(jnp.int32, (BLOCK_LEN, BLOCK_LEN), 0)
    cols = lax.broadcasted_iota(jnp.int32, (BLOCK_LEN, BLOCK_LEN), 1)
    after = jnp.where(rows > cols, 1.0, 0.0).astype(F32)
    drow = lax.broadcasted_iota(jnp.int32, (DEC, DEC), 0)
    dcol = lax.broadcasted_iota(jnp.int32, (DEC, DEC), 1)
    lane = lax.broadcasted_iota(jnp.int32, (DEC, 8), 1)
    grow = lax.broadcasted_iota(jnp.int32, (ROWS, BLOCK_LEN), 0)
    gcol = lax.broadcasted_iota(jnp.int32, (ROWS, BLOCK_LEN), 1)
    live = (gcol <= grow) | (grow >= BLOCK_LEN)

    for n in range(TWO):
        req = req_of[pl.program_id(0) * TWO + n]
        tokens = slice(n * BLOCK_LEN, (n + 1) * BLOCK_LEN)
        step = dt[n]
        decay = step * rate
        left_over = jnp.dot(decay, after, precision=HIGH, preferred_element_type=F32)
        rise = jnp.exp(left_over)
        tail = jnp.exp(-left_over) * step
        whole_fade = jnp.exp(-jnp.sum(decay, axis=1, keepdims=True))
        both = jnp.concatenate([c[tokens], dc[req]], axis=0)
        cross = dot_nt(db[req], dc[req])
        same = jnp.sum(jnp.where(drow == dcol, cross, 0.0), axis=0, keepdims=True)
        prior = jnp.sum(jnp.where(drow + 1 == dcol, cross, 0.0), axis=0, keepdims=True)
        keep = jnp.exp(-dd[req] * rate)
        keep_all = keep * jnp.exp(-dprev[req] * rate)
        columns[n, :, 0:64] = thirds(rise)
        columns[n, :, 64:128] = thirds(tail)
        columns[n, :, 128:144] = thirds(keep_all)
        columns[n, :, 144:160] = thirds(dd[req] * same + skip[...])
        columns[n, :, 160:176] = thirds(keep * dprev[req] * prior)
        columns[n, :, 176:184] = thirds(
            jnp.where(lane == 0, whole_fade, jnp.where(lane == 1, skip[...], 0.0))
        )
        wide = dot_tn(columns[n, :, 0:192].astype(BF16), expand[...])
        rise_w, tail_w = wide[0:64], wide[64:128]
        keep_w, own_w, prior_w = wide[128:144], wide[144:160], wide[160:176]
        skip_w = wide[177:178]
        fade[n] = wide[176:184]

        xf = x[tokens].astype(F32)
        scaled = (xf * tail_w).astype(BF16)
        gram = jnp.where(live, dot_nt(both, b[tokens]), 0.0)
        high = gram.astype(BF16).astype(F32)
        gram2 = jnp.concatenate([high, gram - high], axis=1).astype(BF16)
        inner = dot(gram2, jnp.concatenate([scaled, scaled], axis=0))
        growth[n] = dot_tn(b[tokens], scaled)
        both32 = both.astype(F32)
        left[n] = jnp.concatenate([both32, both32], axis=1).astype(BF16)

        gate = silu(z[tokens].astype(F32))
        base[n, 0:BLOCK_LEN] = (inner[0:BLOCK_LEN] * rise_w + skip_w * xf) * gate
        slope[n, 0:BLOCK_LEN] = rise_w * gate
        dxf = dx[req].astype(F32)
        dgate = silu(dz[req].astype(F32))
        dy = keep_w * inner[BLOCK_LEN:ROWS] + own_w * dxf + prior_w * pltpu.roll(dxf, 1, 0)
        base[n, BLOCK_LEN:ROWS] = dy * dgate
        slope[n, BLOCK_LEN:ROWS] = keep_w * dgate


def expand_matrix():
    out = np.zeros((3, 16, WIDTH), np.float32)
    for head in range(LOCAL):
        out[:, head, head * HEAD_DIM : (head + 1) * HEAD_DIM] = 1.0
    return out.reshape(48, WIDTH).astype(ml_dtypes.bfloat16)


def before(req_of, x, z, b, c, dt, rates, skip, dx, dz, db, dc, dd, dprev):
    def block(*shape):
        return pl.BlockSpec(shape, lambda i, req: (i,) + (0,) * (len(shape) - 1))

    def fixed(*shape):
        return pl.BlockSpec(shape, lambda i, req: (0,) * len(shape))

    return pl.pallas_call(
        before_kernel,
        grid_spec=pltpu.PrefetchScalarGridSpec(
            num_scalar_prefetch=1,
            grid=(NBLK // TWO,),
            in_specs=[
                block(TWO * BLOCK_LEN, WIDTH),
                block(TWO * BLOCK_LEN, WIDTH),
                block(TWO * BLOCK_LEN, STATE),
                block(TWO * BLOCK_LEN, STATE),
                block(TWO, 16, BLOCK_LEN),
                fixed(16, 1),
                fixed(16, 1),
                fixed(REQS, DEC, WIDTH),
                fixed(REQS, DEC, WIDTH),
                fixed(REQS, DEC, STATE),
                fixed(REQS, DEC, STATE),
                fixed(REQS, 16, DEC),
                fixed(REQS, 16, DEC),
                fixed(48, WIDTH),
            ],
            out_specs=[
                block(TWO, ROWS, WIDTH),
                block(TWO, ROWS, WIDTH),
                block(TWO, STATE, WIDTH),
                block(TWO, ROWS, 2 * STATE),
                block(TWO, 8, WIDTH),
            ],
            scratch_shapes=[pltpu.VMEM((TWO, 48, 256), F32)],
        ),
        out_shape=[
            jax.ShapeDtypeStruct((NBLK, ROWS, WIDTH), F32),
            jax.ShapeDtypeStruct((NBLK, ROWS, WIDTH), F32),
            jax.ShapeDtypeStruct((NBLK, STATE, WIDTH), F32),
            jax.ShapeDtypeStruct((NBLK, ROWS, 2 * STATE), BF16),
            jax.ShapeDtypeStruct((NBLK, 8, WIDTH), F32),
        ],
        compiler_params=params(60),
        cost_estimate=pl.CostEstimate(
            flops=NBLK * 2 * 500 * 128 * WIDTH, bytes_accessed=32 << 20, transcendentals=3 << 20
        ),
        name="before",
    )(req_of, x, z, b, c, dt, rates, skip, dx, dz, db, dc, dd, dprev, jnp.asarray(expand_matrix()))


def through_kernel(
    req_of, begins, loc, short, pieces, instead, base, slope, growth, left, fade,
    values, sampled_values, spread, state, first, sums, sem,
):
    step = pl.program_id(0)

    @pl.when(step == 0)
    def _():
        state[...] = jnp.zeros_like(state)

        @pl.when(short[0] == 0)
        def _():
            for n in range(REQS * QUARTERS):
                pltpu.make_async_copy(pieces.at[loc[n]], first.at[n], sem).start()

        @pl.when(short[0] != 0)
        def _():
            for n in range(REQS * QUARTERS):
                pltpu.make_async_copy(instead.at[n], first.at[n], sem).start()

        pltpu.make_async_copy(first, first, sem).wait()

    lane = lax.broadcasted_iota(jnp.int32, (1, 128), 1)
    parts = [jnp.zeros((ROWS, 128), F32)] * FOUR
    for lanes in TILES:
        now = state[:, lanes]
        width = lanes.stop - lanes.start
        for n in range(FOUR):
            k = step * FOUR + n
            req = req_of[k]
            start = first[pl.ds(req * QUARTERS, QUARTERS), :, lanes]
            start = start.reshape(STATE, width).astype(F32)
            faded = jnp.where(begins[k] == 1, start, now) * fade[n, 0:1, lanes]
            high = faded.astype(BF16)
            low = (faded - high.astype(F32)).astype(BF16)
            out = dot(left[n], jnp.concatenate([high, low], axis=0))
            now = faded + growth[n, :, lanes]
            value = base[n, :, lanes] + slope[n, :, lanes] * out
            values[n * BLOCK_LEN : (n + 1) * BLOCK_LEN, lanes] = value[0:BLOCK_LEN]
            sampled_values[pl.ds(pl.multiple_of(req * DEC, DEC), DEC), lanes] = value[
                BLOCK_LEN:ROWS
            ]
            square = value * value
            for tile in range(0, width, 128):
                parts[n] = parts[n] + square[:, tile : tile + 128]
        state[:, lanes] = now
    for n in range(FOUR):
        req = req_of[step * FOUR + n]
        total = jnp.sum(parts[n].T, axis=0, keepdims=True)
        tokens = jnp.concatenate([total[:, 0:BLOCK_LEN]] * 2, axis=1)
        row = step * (FOUR // 2) + n // 2
        sums[pl.ds(row, 1)] = jnp.where(lane >> 6 == n % 2, tokens, sums[pl.ds(row, 1)])
        sampled = jnp.concatenate([total[:, BLOCK_LEN:ROWS]] * 8, axis=1)
        row = NBLK // 2 + (req >> 3)
        sums[pl.ds(row, 1)] = jnp.where(lane >> 4 == (req & 7), sampled, sums[pl.ds(row, 1)])

    @pl.when(step == NBLK // FOUR - 1)
    def _():
        for device in range(8):
            spread[device] = sums[...]


def through(req_of, begins, loc, short, pieces, instead, base, slope, growth, left, fade):
    def block(*shape):
        return pl.BlockSpec(shape, lambda i, *_: (i,) + (0,) * (len(shape) - 1))

    def fixed(*shape):
        return pl.BlockSpec(shape, lambda i, *_: (0,) * len(shape))

    anywhere = pl.BlockSpec(memory_space=pl.ANY)
    return pl.pallas_call(
        through_kernel,
        grid_spec=pltpu.PrefetchScalarGridSpec(
            num_scalar_prefetch=4,
            grid=(NBLK // FOUR,),
            in_specs=[
                anywhere,
                anywhere,
                block(FOUR, ROWS, WIDTH),
                block(FOUR, ROWS, WIDTH),
                block(FOUR, STATE, WIDTH),
                block(FOUR, ROWS, 2 * STATE),
                block(FOUR, 8, WIDTH),
            ],
            out_specs=[
                block(FOUR * BLOCK_LEN, WIDTH),
                fixed(REQS * DEC, WIDTH),
                fixed(8, NBLK // 2 + 2, 128),
            ],
            scratch_shapes=[
                pltpu.VMEM((STATE, WIDTH), F32),
                pltpu.VMEM((REQS * QUARTERS, PIECE, WIDTH), BF16),
                pltpu.VMEM((NBLK // 2 + 2, 128), F32),
                pltpu.SemaphoreType.DMA,
            ],
        ),
        out_shape=[
            jax.ShapeDtypeStruct((TOKS, WIDTH), F32),
            jax.ShapeDtypeStruct((REQS * DEC, WIDTH), F32),
            jax.ShapeDtypeStruct((8, NBLK // 2 + 2, 128), F32),
        ],
        compiler_params=params(62),
        name="through",
    )(req_of, begins, loc, short, pieces, instead, base, slope, growth, left, fade)


def finish_kernel(sums, values, sampled_values, gain, out, dec):
    i = pl.program_id(0)
    last = TOKS // WIDE - 1

    def put(total, source, target):
        scale = lax.rsqrt(total / D_INNER + 1e-05)
        for part in range(source.shape[0] // 128):
            rows = slice(part * 128, part * 128 + 128)
            wide = jnp.broadcast_to(scale[part : part + 1], (128, 128)).T
            for tile in range(WIDTH // 128):
                lanes = slice(tile * 128, (tile + 1) * 128)
                target(rows, lanes, source[rows, lanes] * wide * gain[:, lanes])

    def token(rows, lanes, value):
        out[rows, lanes] = value.astype(BF16)

    def sample(rows, lanes, value):
        first = rows.start // DEC
        dec[first : first + 8, :, :, lanes] = value.reshape(8, 8, 2, 128).astype(BF16)

    for step in range(last + 1):

        @pl.when(i == step)
        def _():
            first = step * WIDE // 128
            put(jnp.sum(sums[:, first : first + WIDE // 128], axis=0), values, token)

    @pl.when(i == last + 1)
    def _():
        put(jnp.sum(sums[:, TOKS // 128 :], axis=0), sampled_values, sample)


def finish(sums, values, sampled_values, gain):
    last = TOKS // WIDE - 1
    return pl.pallas_call(
        finish_kernel,
        grid=(last + 2,),
        in_specs=[
            pl.BlockSpec((8, NBLK // 2 + 2, 128), lambda i: (0, 0, 0)),
            pl.BlockSpec((WIDE, WIDTH), lambda i: (jnp.minimum(i, last), 0)),
            pl.BlockSpec((REQS * DEC, WIDTH), lambda i: (0, 0)),
            pl.BlockSpec((1, WIDTH), lambda i: (0, 0)),
        ],
        out_specs=[
            pl.BlockSpec((WIDE, WIDTH), lambda i: (jnp.minimum(i, last), 0)),
            pl.BlockSpec((REQS, 8, 2, WIDTH), lambda i: (0, 0, 0, 0)),
        ],
        out_shape=[
            jax.ShapeDtypeStruct((TOKS, WIDTH), BF16),
            jax.ShapeDtypeStruct((REQS, 8, 2, WIDTH), BF16),
        ],
        compiler_params=params(60),
        name="finish",
    )(sums, values, sampled_values, gain)


def owner_ranks(owners):
    count = owners.shape[-1]
    same = owners[..., :, None] == owners[..., None, :]
    rows = lax.broadcasted_iota(jnp.int32, (count, count), 0)
    cols = lax.broadcasted_iota(jnp.int32, (count, count), 1)
    return jnp.sum(jnp.where(same & (cols < rows), 1, 0), axis=-1).astype(jnp.int32)


def fetch_all(owners, slots, own):
    wanted = owners * CAP + owner_ranks(owners)
    grid = lax.broadcasted_iota(jnp.int32, (1, OWNERS * CAP), 1)
    table = jnp.sum(jnp.where(wanted[:, None] == grid, slots[:, None], 0), axis=0)
    table = lax.all_to_all(
        table.reshape(OWNERS, CAP), "req", split_axis=0, concat_axis=0, tiled=True
    ).reshape(-1)
    quarter = lax.broadcasted_iota(jnp.int32, (1, QUARTERS), 1)
    rows = jnp.take(own, table[:, None] + REQS * quarter, axis=0)
    arrived = lax.all_to_all(rows, "req", split_axis=0, concat_axis=0, tiled=True)
    arrived = arrived.reshape(OWNERS * CAP * QUARTERS, PIECE, WIDTH)
    mine = jnp.take(arrived, (wanted[:, None] * QUARTERS + quarter).reshape(-1), axis=0)
    rest = jnp.zeros((OWNERS * PLACES - REQS * QUARTERS, PIECE, WIDTH), BF16)
    return jnp.concatenate([mine, rest], axis=0)


def moves(dy, dx, dcore):
    return [
        (
            (y * 4 + x) * 2 + core,
            (((y + dy) % 4) * 4 + (x + dx) % 4) * 2 + (core + dcore) % 2,
        )
        for y in range(4)
        for x in range(4)
        for core in range(2)
    ]


def exchange(value, axis):
    return lax.all_to_all(value, axis, split_axis=0, concat_axis=0, tiled=True)


def on_device(
    features,
    gate_input,
    input_map,
    output_map,
    head_step_sizes,
    log_rate,
    skip_gain,
    norm_gain,
    cache_states,
    hit_owner,
    hit_slot,
    suffix_blocks,
    dec_features,
    dec_gate,
    dec_input_map,
    dec_output_map,
    dec_step_size,
):
    group = lax.axis_index("samp") * LOCAL // (HEADS // GROUPS)
    owners = hit_owner[:, 0]

    table, loc, own, *quarters = prepare(owners, hit_slot, cache_states)
    near = [
        lax.ppermute(quarters[q], "req", moves(*SHIFTS[q], 0)) for q in range(QUARTERS)
    ]
    peer = lax.ppermute(own, "req", moves(0, 0, 1))
    asked = exchange(table, "req")
    short = jnp.max(asked[:, PLACES])
    sent = lax.cond(
        short > 0,
        lambda: fetch_all(owners, hit_slot, own.reshape(QUARTERS * REQS, PIECE, WIDTH)),
        lambda: collect(asked, own, peer, near),
    )
    pieces = exchange(sent, "req")

    lens = suffix_blocks[0]
    ends = jnp.cumsum(lens)
    index = lax.broadcasted_iota(jnp.int32, (NBLK, REQS), 0)
    req_of = jnp.sum(jnp.where(ends[None, :] <= index, 1, 0), axis=1).astype(jnp.int32)
    begins = jnp.any((ends - lens)[None, :] == index, axis=1).astype(jnp.int32)
    b_rows = lax.dynamic_slice_in_dim(input_map, group * STATE, STATE, 1)
    c_rows = lax.dynamic_slice_in_dim(output_map, group * STATE, STATE, 1)
    db = lax.dynamic_slice_in_dim(dec_input_map, group * STATE, STATE, 3)
    dc = lax.dynamic_slice_in_dim(dec_output_map, group * STATE, STATE, 3)
    pad = ((0, 0), (0, 16 - LOCAL), (0, 0))
    dt = jnp.transpose(head_step_sizes.reshape(LOCAL, NBLK, BLOCK_LEN), (1, 0, 2))
    dd = jnp.transpose(dec_step_size, (1, 0, 2, 3))
    dprev = jnp.concatenate([jnp.zeros_like(dd[..., :1]), dd[..., :1]], axis=3)
    tall = ((0, 16 - LOCAL), (0, 0))
    base, slope, growth, left, fade = before(
        req_of,
        features,
        gate_input,
        b_rows,
        c_rows,
        jnp.pad(dt, pad),
        jnp.pad(log_rate[:, None], tall),
        jnp.pad(skip_gain[:, None], tall),
        dec_features.reshape(REQS, DEC, WIDTH),
        dec_gate.reshape(REQS, DEC, WIDTH),
        db.reshape(REQS, DEC, STATE),
        dc.reshape(REQS, DEC, STATE),
        jnp.pad(dd.reshape(REQS, LOCAL, DEC), pad),
        jnp.pad(dprev.reshape(REQS, LOCAL, DEC), pad),
    )

    values, sampled_values, sums = through(
        req_of, begins, loc, short[None], pieces, sent, base, slope, growth, left, fade
    )
    totals = exchange(sums, "samp")
    prefill_out, decode_out = finish(totals, values, sampled_values, norm_gain[None])
    return (prefill_out, decode_out)


def solution(mesh):
    return jax.shard_map(
        on_device,
        mesh=mesh,
        in_specs=(
            P("req", "samp"),
            P("req", "samp"),
            P("req", None),
            P("req", None),
            P("samp", "req"),
            P("samp"),
            P("samp"),
            P("samp"),
            P("req", "samp", None),
            P("req", None),
            P("req"),
            P("req", None),
            P("req", None, None, "samp"),
            P("req", None, None, "samp"),
            P("req", None, None, None),
            P("req", None, None, None),
            P("samp", "req", None, None),
        ),
        out_specs=(P("req", "samp"), P("req", None, None, "samp")),
        check_vma=False,
    )
```

```python
import jax
import jax.numpy as jnp
import ml_dtypes
import numpy as np
from jax import lax
from jax.experimental import pallas as pl
from jax.experimental.pallas import tpu as pltpu
from jax.sharding import PartitionSpec as P

HEADS = 112
HEAD_DIM = 64
STATE = 64
GROUPS = 2
BLOCK_LEN = 64
CAP = 2
STEPS = 2
D_INNER = 7168

LOCAL = 14
WIDTH = LOCAL * HEAD_DIM
REQS = 16
OWNERS = 32
NBLK = 24
TOKS = NBLK * BLOCK_LEN
DEC = 16
ROWS = BLOCK_LEN + DEC
QUARTERS = 4
PIECE = STATE // QUARTERS
TILES = tuple(slice(i, min(i + 256, WIDTH)) for i in range(0, WIDTH, 256))
WIDE = 768
TWO = 2
FOUR = 4
PLACES = 3
SHIFTS = ((0, 1), (0, 3), (1, 0))
NEAR = len(SHIFTS)

F32 = jnp.float32
BF16 = jnp.bfloat16
HIGH = lax.Precision.HIGHEST


def dot(a, b):
    return jnp.dot(a, b, preferred_element_type=F32)


def dot_nt(a, b):
    return lax.dot_general(a, b, (((1,), (1,)), ((), ())), preferred_element_type=F32)


def dot_tn(a, b):
    return lax.dot_general(a, b, (((0,), (0,)), ((), ())), preferred_element_type=F32)


def params(mib):
    return pltpu.CompilerParams(vmem_limit_bytes=mib << 20)


def spread_matrix():
    out = np.zeros((2, 32, REQS, REQS, HEAD_DIM), np.float32)
    for parity in range(2):
        for i in range(32):
            for slot in range(REQS):
                out[parity, i, slot, slot, 2 * i + parity] = 1.0
    return out.reshape(1024, 1024).astype(ml_dtypes.bfloat16)


def shifted(device, q):
    y, x, core = device >> 3, (device >> 1) & 3, device & 1
    dy = jnp.where(q == 2, 1, 0)
    dx = jnp.where(q == 0, 1, jnp.where(q == 1, 3, 0))
    return (((y + dy) & 3) << 3) + (((x + dx) & 3) << 1) + core


def choices(owner, q):
    return owner, owner ^ 1, shifted(owner, q)


def lightest(load, devices):
    a, b, c = (load[device] for device in devices)
    kind = jnp.where((a <= b) & (a <= c), 0, jnp.where(b <= c, 1, 2))
    device = jnp.where(kind == 0, devices[0], jnp.where(kind == 1, devices[1], devices[2]))
    return kind, device, jnp.minimum(a, jnp.minimum(b, c))


def make_plan(owners, slots, table, loc, load, held, seen, origin, queue, late):
    for device in range(OWNERS):
        load[device] = 0
        for place in range(PLACES):
            table[device, place] = 0
    for n in range(REQS * QUARTERS):
        loc[n] = 0

    def put(ball, kind, device, place):
        request, q = ball & 15, ball >> 4
        held[device * PLACES + place] = ball
        loc[request * QUARTERS + q] = device * PLACES + place
        table[device, place] = (kind << 6) + (q << 4) + slots[request]

    waiting = jnp.int32(0)
    for q in range(QUARTERS):
        for request in range(REQS):
            kind, best, room = lightest(load, choices(owners[request], q))
            fits = room < PLACES

            @pl.when(fits)
            def _():
                put((q << 4) + request, kind, best, room)
                load[best] = room + 1

            @pl.when(jnp.logical_not(fits))
            def _():
                late[waiting] = (q << 4) + request

            waiting = waiting + jnp.where(fits, 0, 1)

    def place_late(n, failed):
        ball = late[n]
        for device in range(OWNERS):
            seen[device] = 0

        def visit(options, source, state):
            tail, found = state
            for kind in range(3):
                device = options[kind]
                fresh = (seen[device] == 0) & (found < 0)

                @pl.when(fresh)
                def _():
                    seen[device] = 1
                    origin[device] = (source << 2) + kind
                    queue[tail] = device

                tail = tail + jnp.where(fresh, 1, 0)
                found = jnp.where(fresh & (load[device] < PLACES), device, found)
            return tail, found

        root = OWNERS * PLACES
        start = visit(choices(owners[ball & 15], ball >> 4), root, (jnp.int32(0), jnp.int32(-1)))

        def search(state):
            head, tail, found = state
            device = queue[head]
            for place in range(PLACES):
                spot = device * PLACES + place
                other = held[spot]
                tail, found = visit(choices(owners[other & 15], other >> 4), spot, (tail, found))
            return head + 1, tail, found

        _, _, found = lax.while_loop(
            lambda state: (state[0] < state[1]) & (state[2] < 0),
            search,
            (jnp.int32(0),) + start,
        )

        @pl.when(found >= 0)
        def _():
            room = load[found]
            load[found] = room + 1

            def back(state):
                device, place = state
                source, kind = origin[device] >> 2, origin[device] & 3
                first = source == root
                moved = jnp.where(first, ball, held[jnp.minimum(source, root - 1)])
                put(moved, kind, device, place)
                above = (source * 43) >> 7
                return jnp.where(first, -1, above), source - above * PLACES

            lax.while_loop(lambda state: state[0] >= 0, back, (found, room))

        return failed | jnp.where(found < 0, 1, 0)

    failed = lax.fori_loop(0, waiting, place_late, jnp.int32(0))
    for device in range(OWNERS):
        table[device, PLACES] = failed


def prepare_kernel(
    owners, slots, far_cache, far_spread,
    table, loc, whole, part0, part1, part2,
    cache, spread, turned, load, held, seen, origin, queue, late, sems,
):
    copies = (
        pltpu.make_async_copy(far_cache, cache, sems.at[0]),
        pltpu.make_async_copy(far_spread, spread, sems.at[1]),
    )
    for copy in copies:
        copy.start()
    make_plan(owners, slots, table, loc, load, held, seen, origin, queue, late)
    for copy in copies:
        copy.wait()
    parts = (part0, part1, part2)
    for head in range(LOCAL):
        for chunk in range(4):
            tiles = [
                cache[head, :, (8 * chunk + i) * 128 : (8 * chunk + i + 1) * 128] for i in range(8)
            ]
            block = jnp.concatenate(tiles, axis=0).T
            for parity in range(2):
                first = parity * 512 + chunk * 128
                turned[head * 64 : head * 64 + 64, first : first + 128] = block[
                    parity * 64 : parity * 64 + 64
                ]
    low = lax.broadcasted_iota(jnp.int32, (64, 128), 1) < 64
    for four in range(4):
        out = dot(turned[...], spread[:, four * 256 : four * 256 + 256])
        for two in range(2):
            for pair in range(LOCAL // 2):
                even = out[pair * 128 : pair * 128 + 64, two * 128 : two * 128 + 128]
                odd = out[pair * 128 + 64 : pair * 128 + 128, two * 128 : two * 128 + 128]
                first = jnp.where(low, even, pltpu.roll(odd, 64, 1)).astype(BF16)
                second = jnp.where(low, pltpu.roll(even, 64, 1), odd).astype(BF16)
                for one, value in ((0, first), (1, second)):
                    slot = four * 4 + two * 2 + one
                    for q in range(QUARTERS):
                        piece = value[q * PIECE : (q + 1) * PIECE]
                        whole[q, slot, :, pair * 128 : pair * 128 + 128] = piece
                        if q < NEAR:
                            parts[q][slot, :, pair * 128 : pair * 128 + 128] = piece


def prepare(owners, slots, cache):
    smem = pl.BlockSpec(memory_space=pltpu.SMEM)
    vmem = pl.BlockSpec(memory_space=pltpu.VMEM)
    anywhere = pl.BlockSpec(memory_space=pl.ANY)
    piece = jax.ShapeDtypeStruct((REQS, PIECE, WIDTH), BF16)
    return pl.pallas_call(
        prepare_kernel,
        out_shape=[
            jax.ShapeDtypeStruct((OWNERS, 4), jnp.int32),
            jax.ShapeDtypeStruct((REQS * QUARTERS,), jnp.int32),
            jax.ShapeDtypeStruct((QUARTERS, REQS, PIECE, WIDTH), BF16),
        ]
        + [piece] * NEAR,
        in_specs=[smem, smem, anywhere, anywhere],
        out_specs=[smem] * 2 + [vmem] * (1 + NEAR),
        scratch_shapes=[
            pltpu.VMEM((LOCAL, REQS, HEAD_DIM * STATE), BF16),
            pltpu.VMEM((1024, 1024), BF16),
            pltpu.VMEM((LOCAL * 64, 1024), BF16),
            pltpu.SMEM((OWNERS,), jnp.int32),
            pltpu.SMEM((OWNERS * PLACES,), jnp.int32),
            pltpu.SMEM((OWNERS,), jnp.int32),
            pltpu.SMEM((OWNERS,), jnp.int32),
            pltpu.SMEM((OWNERS,), jnp.int32),
            pltpu.SMEM((REQS * QUARTERS,), jnp.int32),
            pltpu.SemaphoreType.DMA((2,)),
        ],
        compiler_params=params(60),
        name="prepare",
    )(owners, slots, jnp.transpose(cache, (1, 0, 2)), jnp.asarray(spread_matrix()))


def collect_kernel(table, own, peer, near0, near1, near2, out, sem):
    near = (near0, near1, near2)

    def each(device, _):
        for place in range(PLACES):
            code = table[device, place]
            kind, q, slot = code >> 6, (code >> 4) & 3, code & 15
            target = out.at[device * PLACES + place]

            @pl.when(kind == 0)
            def _():
                pltpu.make_async_copy(own.at[q, slot], target, sem).start()

            @pl.when(kind == 1)
            def _():
                pltpu.make_async_copy(peer.at[q, slot], target, sem).start()

            for side in range(NEAR):

                @pl.when((kind == 2) & (q == side))
                def _():
                    pltpu.make_async_copy(near[side].at[slot], target, sem).start()

        return 0

    lax.fori_loop(0, OWNERS, each, 0)
    pltpu.make_async_copy(out, out, sem).wait()


def collect(table, own, peer, near):
    vmem = pl.BlockSpec(memory_space=pltpu.VMEM)
    return pl.pallas_call(
        collect_kernel,
        out_shape=jax.ShapeDtypeStruct((OWNERS * PLACES, PIECE, WIDTH), BF16),
        in_specs=[pl.BlockSpec(memory_space=pltpu.SMEM)] + [vmem] * (2 + NEAR),
        out_specs=pl.BlockSpec(memory_space=pl.ANY),
        scratch_shapes=[pltpu.SemaphoreType.DMA],
        compiler_params=params(16),
        name="collect",
    )(table, own, peer, *near)


def silu(value):
    return value / (1.0 + jnp.exp(-value))


def thirds(value):
    high = value.astype(BF16).astype(F32)
    rest = value - high
    mid = rest.astype(BF16).astype(F32)
    return jnp.concatenate([high, mid, rest - mid], axis=0)


def before_kernel(
    req_of, x, z, b, c, dt, rates, skip, dx, dz, db, dc, dd, dprev, expand,
    base, slope, growth, left, fade, columns,
):
    @pl.when(pl.program_id(0) == 0)
    def _():
        columns[...] = jnp.zeros_like(columns)

    rate = jnp.exp(rates[...])
    rows = lax.broadcasted_iota(jnp.int32, (BLOCK_LEN, BLOCK_LEN), 0)
    cols = lax.broadcasted_iota(jnp.int32, (BLOCK_LEN, BLOCK_LEN), 1)
    after = jnp.where(rows > cols, 1.0, 0.0).astype(F32)
    drow = lax.broadcasted_iota(jnp.int32, (DEC, DEC), 0)
    dcol = lax.broadcasted_iota(jnp.int32, (DEC, DEC), 1)
    lane = lax.broadcasted_iota(jnp.int32, (DEC, 8), 1)
    grow = lax.broadcasted_iota(jnp.int32, (ROWS, BLOCK_LEN), 0)
    gcol = lax.broadcasted_iota(jnp.int32, (ROWS, BLOCK_LEN), 1)
    live = (gcol <= grow) | (grow >= BLOCK_LEN)

    for n in range(TWO):
        req = req_of[pl.program_id(0) * TWO + n]
        tokens = slice(n * BLOCK_LEN, (n + 1) * BLOCK_LEN)
        step = dt[n]
        decay = step * rate
        left_over = jnp.dot(decay, after, precision=HIGH, preferred_element_type=F32)
        rise = jnp.exp(left_over)
        tail = jnp.exp(-left_over) * step
        whole_fade = jnp.exp(-jnp.sum(decay, axis=1, keepdims=True))
        both = jnp.concatenate([c[tokens], dc[req]], axis=0)
        cross = dot_nt(db[req], dc[req])
        same = jnp.sum(jnp.where(drow == dcol, cross, 0.0), axis=0, keepdims=True)
        prior = jnp.sum(jnp.where(drow + 1 == dcol, cross, 0.0), axis=0, keepdims=True)
        keep = jnp.exp(-dd[req] * rate)
        keep_all = keep * jnp.exp(-dprev[req] * rate)
        columns[n, :, 0:64] = thirds(rise)
        columns[n, :, 64:128] = thirds(tail)
        columns[n, :, 128:144] = thirds(keep_all)
        columns[n, :, 144:160] = thirds(dd[req] * same + skip[...])
        columns[n, :, 160:176] = thirds(keep * dprev[req] * prior)
        columns[n, :, 176:184] = thirds(
            jnp.where(lane == 0, whole_fade, jnp.where(lane == 1, skip[...], 0.0))
        )
        wide = dot_tn(columns[n, :, 0:192].astype(BF16), expand[...])
        rise_w, tail_w = wide[0:64], wide[64:128]
        keep_w, own_w, prior_w = wide[128:144], wide[144:160], wide[160:176]
        skip_w = wide[177:178]
        fade[n] = wide[176:184]

        xf = x[tokens].astype(F32)
        scaled = (xf * tail_w).astype(BF16)
        gram = jnp.where(live, dot_nt(both, b[tokens]), 0.0)
        high = gram.astype(BF16).astype(F32)
        gram2 = jnp.concatenate([high, gram - high], axis=1).astype(BF16)
        inner = dot(gram2, jnp.concatenate([scaled, scaled], axis=0))
        growth[n] = dot_tn(b[tokens], scaled).astype(BF16)
        both32 = both.astype(F32)
        left[n] = jnp.concatenate([both32, both32], axis=1).astype(BF16)

        gate = silu(z[tokens].astype(F32))
        base[n, 0:BLOCK_LEN] = (inner[0:BLOCK_LEN] * rise_w + skip_w * xf) * gate
        slope[n, 0:BLOCK_LEN] = rise_w * gate
        dxf = dx[req].astype(F32)
        dgate = silu(dz[req].astype(F32))
        dy = keep_w * inner[BLOCK_LEN:ROWS] + own_w * dxf + prior_w * pltpu.roll(dxf, 1, 0)
        base[n, BLOCK_LEN:ROWS] = dy * dgate
        slope[n, BLOCK_LEN:ROWS] = keep_w * dgate


def expand_matrix():
    out = np.zeros((3, 16, WIDTH), np.float32)
    for head in range(LOCAL):
        out[:, head, head * HEAD_DIM : (head + 1) * HEAD_DIM] = 1.0
    return out.reshape(48, WIDTH).astype(ml_dtypes.bfloat16)


def before(req_of, x, z, b, c, dt, rates, skip, dx, dz, db, dc, dd, dprev):
    def block(*shape):
        return pl.BlockSpec(shape, lambda i, req: (i,) + (0,) * (len(shape) - 1))

    def fixed(*shape):
        return pl.BlockSpec(shape, lambda i, req: (0,) * len(shape))

    return pl.pallas_call(
        before_kernel,
        grid_spec=pltpu.PrefetchScalarGridSpec(
            num_scalar_prefetch=1,
            grid=(NBLK // TWO,),
            in_specs=[
                block(TWO * BLOCK_LEN, WIDTH),
                block(TWO * BLOCK_LEN, WIDTH),
                block(TWO * BLOCK_LEN, STATE),
                block(TWO * BLOCK_LEN, STATE),
                block(TWO, 16, BLOCK_LEN),
                fixed(16, 1),
                fixed(16, 1),
                fixed(REQS, DEC, WIDTH),
                fixed(REQS, DEC, WIDTH),
                fixed(REQS, DEC, STATE),
                fixed(REQS, DEC, STATE),
                fixed(REQS, 16, DEC),
                fixed(REQS, 16, DEC),
                fixed(48, WIDTH),
            ],
            out_specs=[
                block(TWO, ROWS, WIDTH),
                block(TWO, ROWS, WIDTH),
                block(TWO, STATE, WIDTH),
                block(TWO, ROWS, 2 * STATE),
                block(TWO, 8, WIDTH),
            ],
            scratch_shapes=[pltpu.VMEM((TWO, 48, 256), F32)],
        ),
        out_shape=[
            jax.ShapeDtypeStruct((NBLK, ROWS, WIDTH), F32),
            jax.ShapeDtypeStruct((NBLK, ROWS, WIDTH), F32),
            jax.ShapeDtypeStruct((NBLK, STATE, WIDTH), BF16),
            jax.ShapeDtypeStruct((NBLK, ROWS, 2 * STATE), BF16),
            jax.ShapeDtypeStruct((NBLK, 8, WIDTH), F32),
        ],
        compiler_params=params(60),
        cost_estimate=pl.CostEstimate(
            flops=NBLK * 2 * 500 * 128 * WIDTH, bytes_accessed=32 << 20, transcendentals=3 << 20
        ),
        name="before",
    )(req_of, x, z, b, c, dt, rates, skip, dx, dz, db, dc, dd, dprev, jnp.asarray(expand_matrix()))


def through_kernel(
    req_of, begins, loc, short, pieces, instead, base, slope, growth, left, fade,
    values, sampled_values, spread, state, first, sums, sem,
):
    step = pl.program_id(0)

    @pl.when(step == 0)
    def _():
        state[...] = jnp.zeros_like(state)

        @pl.when(short[0] == 0)
        def _():
            for n in range(REQS * QUARTERS):
                pltpu.make_async_copy(pieces.at[loc[n]], first.at[n], sem).start()

        @pl.when(short[0] != 0)
        def _():
            for n in range(REQS * QUARTERS):
                pltpu.make_async_copy(instead.at[n], first.at[n], sem).start()

        pltpu.make_async_copy(first, first, sem).wait()

    lane = lax.broadcasted_iota(jnp.int32, (1, 128), 1)
    parts = [jnp.zeros((ROWS, 128), F32)] * FOUR
    for lanes in TILES:
        now = state[:, lanes]
        width = lanes.stop - lanes.start
        for n in range(FOUR):
            k = step * FOUR + n
            req = req_of[k]
            start = first[pl.ds(req * QUARTERS, QUARTERS), :, lanes]
            start = start.reshape(STATE, width).astype(F32)
            faded = jnp.where(begins[k] == 1, start, now) * fade[n, 0:1, lanes]
            high = faded.astype(BF16)
            low = (faded - high.astype(F32)).astype(BF16)
            out = dot(left[n], jnp.concatenate([high, low], axis=0))
            now = faded + growth[n, :, lanes].astype(F32)
            value = base[n, :, lanes] + slope[n, :, lanes] * out
            values[n * BLOCK_LEN : (n + 1) * BLOCK_LEN, lanes] = value[0:BLOCK_LEN]
            sampled_values[pl.ds(pl.multiple_of(req * DEC, DEC), DEC), lanes] = value[
                BLOCK_LEN:ROWS
            ]
            square = value * value
            for tile in range(0, width, 128):
                parts[n] = parts[n] + square[:, tile : tile + 128]
        state[:, lanes] = now
    for n in range(FOUR):
        req = req_of[step * FOUR + n]
        total = jnp.sum(parts[n].T, axis=0, keepdims=True)
        tokens = jnp.concatenate([total[:, 0:BLOCK_LEN]] * 2, axis=1)
        row = step * (FOUR // 2) + n // 2
        sums[pl.ds(row, 1)] = jnp.where(lane >> 6 == n % 2, tokens, sums[pl.ds(row, 1)])
        sampled = jnp.concatenate([total[:, BLOCK_LEN:ROWS]] * 8, axis=1)
        row = NBLK // 2 + (req >> 3)
        sums[pl.ds(row, 1)] = jnp.where(lane >> 4 == (req & 7), sampled, sums[pl.ds(row, 1)])

    @pl.when(step == NBLK // FOUR - 1)
    def _():
        for device in range(8):
            spread[device] = sums[...]


def through(req_of, begins, loc, short, pieces, instead, base, slope, growth, left, fade):
    def block(*shape):
        return pl.BlockSpec(shape, lambda i, *_: (i,) + (0,) * (len(shape) - 1))

    def fixed(*shape):
        return pl.BlockSpec(shape, lambda i, *_: (0,) * len(shape))

    anywhere = pl.BlockSpec(memory_space=pl.ANY)
    return pl.pallas_call(
        through_kernel,
        grid_spec=pltpu.PrefetchScalarGridSpec(
            num_scalar_prefetch=4,
            grid=(NBLK // FOUR,),
            in_specs=[
                anywhere,
                anywhere,
                block(FOUR, ROWS, WIDTH),
                block(FOUR, ROWS, WIDTH),
                block(FOUR, STATE, WIDTH),
                block(FOUR, ROWS, 2 * STATE),
                block(FOUR, 8, WIDTH),
            ],
            out_specs=[
                block(FOUR * BLOCK_LEN, WIDTH),
                fixed(REQS * DEC, WIDTH),
                fixed(8, NBLK // 2 + 2, 128),
            ],
            scratch_shapes=[
                pltpu.VMEM((STATE, WIDTH), F32),
                pltpu.VMEM((REQS * QUARTERS, PIECE, WIDTH), BF16),
                pltpu.VMEM((NBLK // 2 + 2, 128), F32),
                pltpu.SemaphoreType.DMA,
            ],
        ),
        out_shape=[
            jax.ShapeDtypeStruct((TOKS, WIDTH), F32),
            jax.ShapeDtypeStruct((REQS * DEC, WIDTH), F32),
            jax.ShapeDtypeStruct((8, NBLK // 2 + 2, 128), F32),
        ],
        compiler_params=params(62),
        name="through",
    )(req_of, begins, loc, short, pieces, instead, base, slope, growth, left, fade)


def finish_kernel(sums, values, sampled_values, gain, out, dec):
    i = pl.program_id(0)
    last = TOKS // WIDE - 1

    def put(total, source, target):
        scale = lax.rsqrt(total / D_INNER + 1e-05)
        for part in range(source.shape[0] // 128):
            rows = slice(part * 128, part * 128 + 128)
            wide = jnp.broadcast_to(scale[part : part + 1], (128, 128)).T
            for tile in range(WIDTH // 128):
                lanes = slice(tile * 128, (tile + 1) * 128)
                target(rows, lanes, source[rows, lanes] * wide * gain[:, lanes])

    def token(rows, lanes, value):
        out[rows, lanes] = value.astype(BF16)

    def sample(rows, lanes, value):
        first = rows.start // DEC
        dec[first : first + 8, :, :, lanes] = value.reshape(8, 8, 2, 128).astype(BF16)

    for step in range(last + 1):

        @pl.when(i == step)
        def _():
            first = step * WIDE // 128
            put(jnp.sum(sums[:, first : first + WIDE // 128], axis=0), values, token)

    @pl.when(i == last + 1)
    def _():
        put(jnp.sum(sums[:, TOKS // 128 :], axis=0), sampled_values, sample)


def finish(sums, values, sampled_values, gain):
    last = TOKS // WIDE - 1
    return pl.pallas_call(
        finish_kernel,
        grid=(last + 2,),
        in_specs=[
            pl.BlockSpec((8, NBLK // 2 + 2, 128), lambda i: (0, 0, 0)),
            pl.BlockSpec((WIDE, WIDTH), lambda i: (jnp.minimum(i, last), 0)),
            pl.BlockSpec((REQS * DEC, WIDTH), lambda i: (0, 0)),
            pl.BlockSpec((1, WIDTH), lambda i: (0, 0)),
        ],
        out_specs=[
            pl.BlockSpec((WIDE, WIDTH), lambda i: (jnp.minimum(i, last), 0)),
            pl.BlockSpec((REQS, 8, 2, WIDTH), lambda i: (0, 0, 0, 0)),
        ],
        out_shape=[
            jax.ShapeDtypeStruct((TOKS, WIDTH), BF16),
            jax.ShapeDtypeStruct((REQS, 8, 2, WIDTH), BF16),
        ],
        compiler_params=params(60),
        name="finish",
    )(sums, values, sampled_values, gain)


def owner_ranks(owners):
    count = owners.shape[-1]
    same = owners[..., :, None] == owners[..., None, :]
    rows = lax.broadcasted_iota(jnp.int32, (count, count), 0)
    cols = lax.broadcasted_iota(jnp.int32, (count, count), 1)
    return jnp.sum(jnp.where(same & (cols < rows), 1, 0), axis=-1).astype(jnp.int32)


def fetch_all(owners, slots, own):
    wanted = owners * CAP + owner_ranks(owners)
    grid = lax.broadcasted_iota(jnp.int32, (1, OWNERS * CAP), 1)
    table = jnp.sum(jnp.where(wanted[:, None] == grid, slots[:, None], 0), axis=0)
    table = lax.all_to_all(
        table.reshape(OWNERS, CAP), "req", split_axis=0, concat_axis=0, tiled=True
    ).reshape(-1)
    quarter = lax.broadcasted_iota(jnp.int32, (1, QUARTERS), 1)
    rows = jnp.take(own, table[:, None] + REQS * quarter, axis=0)
    arrived = lax.all_to_all(rows, "req", split_axis=0, concat_axis=0, tiled=True)
    arrived = arrived.reshape(OWNERS * CAP * QUARTERS, PIECE, WIDTH)
    mine = jnp.take(arrived, (wanted[:, None] * QUARTERS + quarter).reshape(-1), axis=0)
    rest = jnp.zeros((OWNERS * PLACES - REQS * QUARTERS, PIECE, WIDTH), BF16)
    return jnp.concatenate([mine, rest], axis=0)


def moves(dy, dx, dcore):
    return [
        (
            (y * 4 + x) * 2 + core,
            (((y + dy) % 4) * 4 + (x + dx) % 4) * 2 + (core + dcore) % 2,
        )
        for y in range(4)
        for x in range(4)
        for core in range(2)
    ]


def exchange(value, axis):
    return lax.all_to_all(value, axis, split_axis=0, concat_axis=0, tiled=True)


def on_device(
    features,
    gate_input,
    input_map,
    output_map,
    head_step_sizes,
    log_rate,
    skip_gain,
    norm_gain,
    cache_states,
    hit_owner,
    hit_slot,
    suffix_blocks,
    dec_features,
    dec_gate,
    dec_input_map,
    dec_output_map,
    dec_step_size,
):
    group = lax.axis_index("samp") * LOCAL // (HEADS // GROUPS)
    owners = hit_owner[:, 0]

    table, loc, own, *quarters = prepare(owners, hit_slot, cache_states)
    near = [lax.ppermute(quarters[q], "req", moves(*SHIFTS[q], 0)) for q in range(NEAR)]
    peer = lax.ppermute(own, "req", moves(0, 0, 1))
    asked = exchange(table, "req")
    short = jnp.max(asked[:, PLACES])
    sent = lax.cond(
        short > 0,
        lambda: fetch_all(owners, hit_slot, own.reshape(QUARTERS * REQS, PIECE, WIDTH)),
        lambda: collect(asked, own, peer, near),
    )
    pieces = exchange(sent, "req")

    lens = suffix_blocks[0]
    ends = jnp.cumsum(lens)
    index = lax.broadcasted_iota(jnp.int32, (NBLK, REQS), 0)
    req_of = jnp.sum(jnp.where(ends[None, :] <= index, 1, 0), axis=1).astype(jnp.int32)
    begins = jnp.any((ends - lens)[None, :] == index, axis=1).astype(jnp.int32)
    b_rows = lax.dynamic_slice_in_dim(input_map, group * STATE, STATE, 1)
    c_rows = lax.dynamic_slice_in_dim(output_map, group * STATE, STATE, 1)
    db = lax.dynamic_slice_in_dim(dec_input_map, group * STATE, STATE, 3)
    dc = lax.dynamic_slice_in_dim(dec_output_map, group * STATE, STATE, 3)
    pad = ((0, 0), (0, 16 - LOCAL), (0, 0))
    dt = jnp.transpose(head_step_sizes.reshape(LOCAL, NBLK, BLOCK_LEN), (1, 0, 2))
    dd = jnp.transpose(dec_step_size, (1, 0, 2, 3))
    dprev = jnp.concatenate([jnp.zeros_like(dd[..., :1]), dd[..., :1]], axis=3)
    tall = ((0, 16 - LOCAL), (0, 0))
    base, slope, growth, left, fade = before(
        req_of,
        features,
        gate_input,
        b_rows,
        c_rows,
        jnp.pad(dt, pad),
        jnp.pad(log_rate[:, None], tall),
        jnp.pad(skip_gain[:, None], tall),
        dec_features.reshape(REQS, DEC, WIDTH),
        dec_gate.reshape(REQS, DEC, WIDTH),
        db.reshape(REQS, DEC, STATE),
        dc.reshape(REQS, DEC, STATE),
        jnp.pad(dd.reshape(REQS, LOCAL, DEC), pad),
        jnp.pad(dprev.reshape(REQS, LOCAL, DEC), pad),
    )

    values, sampled_values, sums = through(
        req_of, begins, loc, short[None], pieces, sent, base, slope, growth, left, fade
    )
    totals = exchange(sums, "samp")
    prefill_out, decode_out = finish(totals, values, sampled_values, norm_gain[None])
    return (prefill_out, decode_out)


def solution(mesh):
    return jax.shard_map(
        on_device,
        mesh=mesh,
        in_specs=(
            P("req", "samp"),
            P("req", "samp"),
            P("req", None),
            P("req", None),
            P("samp", "req"),
            P("samp"),
            P("samp"),
            P("samp"),
            P("req", "samp", None),
            P("req", None),
            P("req"),
            P("req", None),
            P("req", None, None, "samp"),
            P("req", None, None, "samp"),
            P("req", None, None, None),
            P("req", None, None, None),
            P("samp", "req", None, None),
        ),
        out_specs=(P("req", "samp"), P("req", None, None, "samp")),
        check_vma=False,
    )
```
